32 devices in a mesh: seq: 8 (over z, x), ch: 4 (over y, core).
Axes of the slice: x: 2, y: 2, z: 4, core: 2. Of those that a mesh axis runs over, the one named last changes fastest.
Arguments:
- tokens: bfloat16 [2048, 8192], P('seq', 'ch'), may hold values from -6 to 6
- proj_weight: bfloat16 [3, 8192, 4096], P(None, None, 'ch'), may hold values from -0.0625 to 0.0625
- short_taps: float32 [3, 7, 4096], P(None, None, 'ch'), may hold values from -2.4 to 2.4
- long_filter: float32 [2048, 4096], P('seq', 'ch'), may hold values from -0.125 to 0.125
- skip_gain: float32 [4096], P('ch'), may hold values from 0.5 to 1.5
Outputs:
- operator_out: bfloat16 [2048, 4096], P('seq', 'ch')
The draws below stay inside these ranges and needn't reach their ends.
All inputs are finite; a program needn't handle non-finite values.
Results may differ from the reference program's by a relative error of at most 0.0064.
Values may be sent and summed in bfloat16 or wider, within the bound.
A program may use at most 128 MiB of HBM per device.

```python
import jax
import jax.numpy as jnp

D = 8192
C = 4096
TAPS = 7
SEQ_LEN = 2048


def block_levels(own_key, shape, cuts, smallest, top_value):
    factor_of, own = 1.0, jax.random.fold_in(own_key, 6)
    for axis_at, parts in cuts:
        heights = jnp.exp(jax.random.uniform(jax.random.fold_in(own, axis_at), (parts,), jnp.float32, smallest / len(cuts), top_value / len(cuts)))
        factor_of = factor_of * jnp.repeat(heights, shape[axis_at] // parts).reshape([-1 if axis == axis_at else 1 for axis in range(len(shape))])
    return factor_of


def scatter_about(rng, dims, deviation, reach, cuts=(), held_as=jnp.bfloat16):
    factor_of = block_levels(rng, dims, cuts, -0.22, 0.18) if cuts else 1.0
    array = jax.random.normal(rng, dims, jnp.float32) * deviation * factor_of
    return jnp.minimum(jnp.maximum(array, -reach), reach).astype(held_as)


def setup_inputs(seed: int = 0) -> dict:
    seeds = jax.random.split(jax.random.key(seed), 6)
    return {
        "tokens": scatter_about(seeds[0], (SEQ_LEN, D), 1.0, 6.0, ((0, 8), (1, 4))),
        "proj_weight": scatter_about(seeds[1], (3, D, C), D ** -0.5, 0.0625, ((2, 4),)),
        "short_taps": scatter_about(seeds[2], (3, TAPS, C), 0.4, 2.4, ((2, 4),), jnp.float32),
        "long_filter": scatter_about(seeds[3], (SEQ_LEN, C), SEQ_LEN ** -0.5, 0.125, ((0, 8), (1, 4)), jnp.float32),
        "skip_gain": jnp.clip(0.5 + 1.0 * jax.random.uniform(seeds[4], (C,), jnp.float32) ** block_levels(seeds[4], (C,), ((0, 4),), -0.2, 0.2), 0.5, 1.5),
    }


def causal_short(projected, taps):
    padding = jnp.zeros((TAPS - 1, projected.shape[1]), projected.dtype)
    padded = jnp.concatenate([padding, projected], 0).astype(jnp.float32)
    result = jnp.zeros(projected.shape, jnp.float32)
    for tap_index in range(TAPS):
        begin = TAPS - 1 - tap_index
        result = result + taps[tap_index] * padded[begin:begin + SEQ_LEN]
    return result


def reference(tokens, proj_weight, short_taps, long_filter, skip_gain):
    filtered = []
    for branch in range(3):
        projected = jnp.dot(tokens, proj_weight[branch], preferred_element_type=jnp.float32).astype(jnp.bfloat16)
        filtered.append(causal_short(projected, short_taps[branch]))
    query_part, key_part, value_part = filtered
    gated_input = key_part * value_part
    fft_length = 2 * SEQ_LEN
    spectrum = jnp.fft.rfft(gated_input, n=fft_length, axis=0) * jnp.fft.rfft(long_filter, n=fft_length, axis=0)
    long_conv = jnp.fft.irfft(spectrum, n=fft_length, axis=0)[:SEQ_LEN]
    return (query_part * (long_conv + skip_gain * gated_input)).astype(jnp.bfloat16)
```

```python
import functools
import math

import jax
import jax.numpy as jnp
import numpy as np
from jax import lax
from jax.experimental import pallas as pl
from jax.experimental.pallas import tpu as pltpu
from jax.sharding import PartitionSpec as P

TAPS = 7
LANES = 128


HIGH = lax.Precision.HIGHEST


def shifted(value, axis, by):
    size = lax.axis_size(axis)
    pairs = [(i, i + by) for i in range(size) if 0 <= i + by < size]
    return lax.ppermute(value, axis, pairs)


def spread_out(values):
    return lax.all_to_all(values, "seq", split_axis=2, concat_axis=1, tiled=True)


def collect_in(values):
    return lax.all_to_all(values, "seq", split_axis=1, concat_axis=2, tiled=True)


def angle_table(first, second, modulus):
    index_prod = first[:, None] * second[None, :] % modulus
    angles = index_prod.astype(jnp.float32) * (2.0 * math.pi / modulus)
    return (jnp.cos(angles), jnp.sin(angles))


def frequency_order(seq_count):
    places = jnp.arange(2 * seq_count, dtype=jnp.int32)
    owner = places // 2
    second = places % 2
    mirror = jnp.where(second == 0, owner, 2 * seq_count - owner)
    return jnp.where(owner == 0, second * seq_count, mirror)


def spread_convolution(signal, kernel):
    row_count = signal.shape[0]
    seq_count = lax.axis_size("seq")
    slice_rows = row_count // seq_count
    seq_total = seq_count * row_count
    fft_length = 2 * seq_total
    seq_index = lax.axis_index("seq")
    stacked = jnp.stack([signal, kernel])[:, None]
    spread = spread_out(stacked)
    freq_outer = frequency_order(seq_count)
    time_outer = jnp.arange(seq_count, dtype=jnp.int32)
    cos_outer, sin_outer = angle_table(freq_outer, time_outer, 2 * seq_count)
    inner_pos = seq_index * slice_rows + jnp.arange(slice_rows, dtype=jnp.int32)
    cos_twist, sin_twist = angle_table(freq_outer, inner_pos, fft_length)
    inner_index = jnp.arange(row_count, dtype=jnp.int32)
    cos_inner, sin_inner = angle_table(inner_index, inner_index, row_count)
    real_part = jnp.einsum("ft,atjc->afjc", cos_outer, spread, precision=HIGH)
    imag_part = -jnp.einsum("ft,atjc->afjc", sin_outer, spread, precision=HIGH)
    twist_cos = cos_twist[None, :, :, None]
    twist_sin = sin_twist[None, :, :, None]
    twisted_real = real_part * twist_cos + imag_part * twist_sin
    twisted_imag = imag_part * twist_cos - real_part * twist_sin
    paired = collect_in(jnp.concatenate([twisted_real, twisted_imag], 0))
    paired_real = paired[:2]
    paired_imag = paired[2:]
    freq_real = jnp.einsum("gt,aptc->apgc", cos_inner, paired_real, precision=HIGH) + jnp.einsum(
        "gt,aptc->apgc", sin_inner, paired_imag, precision=HIGH
    )
    freq_imag = jnp.einsum("gt,aptc->apgc", cos_inner, paired_imag, precision=HIGH) - jnp.einsum(
        "gt,aptc->apgc", sin_inner, paired_real, precision=HIGH
    )
    prod_real = freq_real[0] * freq_real[1] - freq_imag[0] * freq_imag[1]
    prod_imag = freq_real[0] * freq_imag[1] + freq_imag[0] * freq_real[1]
    final_factor = 1.0 / fft_length
    back_real = jnp.einsum("tg,pgc->ptc", cos_inner, prod_real, precision=HIGH) - jnp.einsum(
        "tg,pgc->ptc", sin_inner, prod_imag, precision=HIGH
    )
    back_imag = jnp.einsum("tg,pgc->ptc", cos_inner, prod_imag, precision=HIGH) + jnp.einsum(
        "tg,pgc->ptc", sin_inner, prod_real, precision=HIGH
    )
    returned = spread_out(jnp.stack([back_real, back_imag]))
    back_cos = cos_twist[:, :, None]
    back_sin = sin_twist[:, :, None]
    untwist_real = returned[0] * back_cos - returned[1] * back_sin
    untwist_imag = returned[0] * back_sin + returned[1] * back_cos
    time_values = jnp.einsum("ft,fjc->tjc", cos_outer, untwist_real, precision=HIGH) - jnp.einsum(
        "ft,fjc->tjc", sin_outer, untwist_imag, precision=HIGH
    )
    time_values = time_values * final_factor
    gathered = collect_in(time_values[None])
    return gathered[0, 0]


def transform_tables(blocks, rows):
    index = np.arange(rows)
    angle = 2.0 * np.pi * (index[:, None] * index[None, :] % rows) / rows
    cos, sin = np.cos(angle), np.sin(angle)
    there = np.block([[cos, sin], [-sin, cos]])
    back = np.block([[cos, -sin], [sin, cos]])
    twist = 2.0 * np.pi * np.arange(blocks + 1)[:, None] * index[None, :] / (2 * blocks * rows)
    twist = np.stack([np.cos(twist), np.sin(twist)], 1)[..., None]
    twist = np.broadcast_to(twist, twist.shape[:3] + (LANES,))
    return (
        jnp.asarray(there, jnp.bfloat16),
        jnp.asarray(back, jnp.bfloat16),
        jnp.asarray(twist, jnp.float32),
    )


def weighted(terms):
    total = None
    for factor, array in terms:
        if abs(factor) < 1e-12:
            continue
        if abs(factor - 1.0) < 1e-12:
            total = array if total is None else total + array
        elif abs(factor + 1.0) < 1e-12:
            total = -array if total is None else total - array
        else:
            total = factor * array if total is None else total + factor * array
    return total


def fold(load, blocks):
    half = blocks // 2
    first, middle = load(0), load(half)
    sums, gaps = [], []
    for j in range(1, half):
        low, high = load(j), load(blocks - j)
        sums.append(low + high)
        gaps.append(low - high)
    return first, middle, sums, gaps


def outer_stage(folded, freq, blocks):
    first, middle, sums, gaps = folded
    half = blocks // 2
    even = freq % 2 == 0
    cos_of = lambda j: math.cos(math.pi * freq * j / blocks)
    sin_of = lambda j: math.sin(math.pi * freq * j / blocks)
    with_cos, with_sin = (sums, gaps) if even else (gaps, sums)
    real = weighted(
        [(1.0, first), (cos_of(half), middle)] + [(cos_of(j), with_cos[j - 1]) for j in range(1, half)]
    )
    imag = weighted([(-sin_of(half), middle)] + [(-sin_of(j), with_sin[j - 1]) for j in range(1, half)])
    return real, imag


def twisted_stage(folded, freq, blocks, cos, sin):
    real, imag = outer_stage(folded, freq, blocks)
    if imag is None:
        return jnp.concatenate([real * cos, -(real * sin)], 0).astype(jnp.bfloat16)
    return jnp.concatenate([real * cos + imag * sin, imag * cos - real * sin], 0).astype(jnp.bfloat16)


def local_convolution(blocks, rows, load_signal, load_filter, there, back, twist):
    half = blocks // 2
    signal, filt = fold(load_signal, blocks), fold(load_filter, blocks)
    cos_even, sin_even = [None] * (half + 1), [None] * (half + 1)
    cos_odd, sin_odd = [None] * (half + 1), [None] * (half + 1)
    plus = lambda old, new: new if old is None else (old if new is None else old + new)
    for freq in range(blocks + 1):
        cos, sin = twist[freq, 0], twist[freq, 1]
        stacked = jnp.concatenate(
            [
                twisted_stage(signal, freq, blocks, cos, sin),
                twisted_stage(filt, freq, blocks, cos, sin),
            ],
            1,
        )
        spectrum = jnp.dot(there[...], stacked, preferred_element_type=jnp.float32)
        sig_real, sig_imag = spectrum[:rows, :LANES], spectrum[rows:, :LANES]
        fil_real, fil_imag = spectrum[:rows, LANES:], spectrum[rows:, LANES:]
        scale = (1.0 if freq in (0, blocks) else 2.0) / (2 * blocks * rows)
        product = jnp.concatenate(
            [
                (sig_real * fil_real - sig_imag * fil_imag) * scale,
                (sig_real * fil_imag + sig_imag * fil_real) * scale,
            ],
            0,
        ).astype(jnp.bfloat16)
        values = jnp.dot(back[...], product, preferred_element_type=jnp.float32)
        real, imag = values[:rows], values[rows:]
        out_real, out_imag = real * cos - imag * sin, real * sin + imag * cos
        cos_sum, sin_sum = (cos_even, sin_even) if freq % 2 == 0 else (cos_odd, sin_odd)
        for j in range(half + 1):
            angle = math.pi * freq * j / blocks
            cos_sum[j] = plus(cos_sum[j], weighted([(math.cos(angle), out_real)]))
            sin_sum[j] = plus(sin_sum[j], weighted([(math.sin(angle), out_imag)]))
    minus = lambda left, right: left if right is None else (-right if left is None else left - right)
    result = [None] * blocks
    for j in range(half + 1):
        result[j] = minus(plus(cos_even[j], cos_odd[j]), plus(sin_even[j], sin_odd[j]))
        if 0 < j < half:
            result[blocks - j] = plus(minus(cos_even[j], cos_odd[j]), minus(sin_even[j], sin_odd[j]))
    return result


def convolution_kernel(blocks, rows, signal, filt, there, back, twist, out):
    result = local_convolution(
        blocks,
        rows,
        lambda j: signal[j].astype(jnp.float32),
        lambda j: filt[j].astype(jnp.float32),
        there,
        back,
        twist,
    )
    for j in range(blocks):
        out[j] = result[j].astype(out.dtype)


def narrow_convolution(signal, spread_filter):
    blocks = lax.axis_size("seq")
    rows = signal.shape[0]
    spread_signal = exchange(signal)
    there, back, twist = transform_tables(blocks, rows)
    out = pl.pallas_call(
        functools.partial(convolution_kernel, blocks, rows),
        out_shape=jax.ShapeDtypeStruct((blocks, rows, LANES), jnp.bfloat16),
        in_specs=[pl.BlockSpec(memory_space=pltpu.VMEM)] * 5,
        out_specs=pl.BlockSpec(memory_space=pltpu.VMEM),
        compiler_params=pltpu.CompilerParams(vmem_limit_bytes=48 * 1024 * 1024),
        name="long_convolution",
    )(spread_signal, spread_filter, there, back, twist)
    gathered = lax.all_to_all(out, "seq", split_axis=0, concat_axis=0, tiled=True)
    return jnp.swapaxes(gathered, 0, 1).reshape(signal.shape).astype(jnp.float32)


def exchange(values):
    blocks = lax.axis_size("seq")
    parts = values.astype(jnp.bfloat16).reshape(values.shape[0], blocks, LANES)
    return lax.all_to_all(jnp.swapaxes(parts, 0, 1), "seq", split_axis=0, concat_axis=0, tiled=True)


def per_device(tokens, proj_weight, short_taps, long_filter, skip_gain):
    row_count = tokens.shape[0]
    chan_count = proj_weight.shape[2]
    seq_count = lax.axis_size("seq")
    narrow = chan_count == seq_count * LANES and row_count % 16 == 0 and seq_count % 4 == 0
    if narrow:
        spread_filter = exchange(long_filter)
    projected = jnp.einsum(
        "td,jdc->jtc",
        lax.all_gather(tokens, "ch", axis=1, tiled=True),
        proj_weight,
        preferred_element_type=jnp.float32,
    ).astype(jnp.bfloat16)
    rim_rows = shifted(projected[:, row_count - (TAPS - 1) :], "seq", 1)
    extended = jnp.concatenate([rim_rows, projected], 1)
    filtered = jnp.zeros((3, row_count, chan_count), jnp.float32)
    for tap_index in range(TAPS):
        begin = TAPS - 1 - tap_index
        filtered = filtered + short_taps[:, tap_index][:, None, :] * extended[
            :, begin : begin + row_count
        ].astype(jnp.float32)
    query_part = filtered[0]
    gated_input = filtered[1] * filtered[2]
    if narrow:
        long_conv = narrow_convolution(gated_input, spread_filter)
    else:
        long_conv = spread_convolution(gated_input, long_filter)
    return (query_part * (long_conv + skip_gain * gated_input)).astype(jnp.bfloat16)


def solution(mesh):
    return jax.shard_map(
        per_device,
        mesh=mesh,
        in_specs=(
            P("seq", "ch"),
            P(None, None, "ch"),
            P(None, None, "ch"),
            P("seq", "ch"),
            P("ch"),
        ),
        out_specs=P("seq", "ch"),
        check_vma=False,
    )
```

```python
import functools
import math

import jax
import jax.numpy as jnp
import numpy as np
from jax import lax
from jax.experimental import pallas as pl
from jax.experimental.pallas import tpu as pltpu
from jax.sharding import PartitionSpec as P

TAPS = 7
LANES = 128


HIGH = lax.Precision.HIGHEST


def shifted(value, axis, by):
    size = lax.axis_size(axis)
    pairs = [(i, i + by) for i in range(size) if 0 <= i + by < size]
    return lax.ppermute(value, axis, pairs)


def spread_out(values):
    return lax.all_to_all(values, "seq", split_axis=2, concat_axis=1, tiled=True)


def collect_in(values):
    return lax.all_to_all(values, "seq", split_axis=1, concat_axis=2, tiled=True)


def angle_table(first, second, modulus):
    index_prod = first[:, None] * second[None, :] % modulus
    angles = index_prod.astype(jnp.float32) * (2.0 * math.pi / modulus)
    return (jnp.cos(angles), jnp.sin(angles))


def frequency_order(seq_count):
    places = jnp.arange(2 * seq_count, dtype=jnp.int32)
    owner = places // 2
    second = places % 2
    mirror = jnp.where(second == 0, owner, 2 * seq_count - owner)
    return jnp.where(owner == 0, second * seq_count, mirror)


def spread_convolution(signal, kernel):
    row_count = signal.shape[0]
    seq_count = lax.axis_size("seq")
    slice_rows = row_count // seq_count
    seq_total = seq_count * row_count
    fft_length = 2 * seq_total
    seq_index = lax.axis_index("seq")
    stacked = jnp.stack([signal, kernel])[:, None]
    spread = spread_out(stacked)
    freq_outer = frequency_order(seq_count)
    time_outer = jnp.arange(seq_count, dtype=jnp.int32)
    cos_outer, sin_outer = angle_table(freq_outer, time_outer, 2 * seq_count)
    inner_pos = seq_index * slice_rows + jnp.arange(slice_rows, dtype=jnp.int32)
    cos_twist, sin_twist = angle_table(freq_outer, inner_pos, fft_length)
    inner_index = jnp.arange(row_count, dtype=jnp.int32)
    cos_inner, sin_inner = angle_table(inner_index, inner_index, row_count)
    real_part = jnp.einsum("ft,atjc->afjc", cos_outer, spread, precision=HIGH)
    imag_part = -jnp.einsum("ft,atjc->afjc", sin_outer, spread, precision=HIGH)
    twist_cos = cos_twist[None, :, :, None]
    twist_sin = sin_twist[None, :, :, None]
    twisted_real = real_part * twist_cos + imag_part * twist_sin
    twisted_imag = imag_part * twist_cos - real_part * twist_sin
    paired = collect_in(jnp.concatenate([twisted_real, twisted_imag], 0))
    paired_real = paired[:2]
    paired_imag = paired[2:]
    freq_real = jnp.einsum("gt,aptc->apgc", cos_inner, paired_real, precision=HIGH) + jnp.einsum(
        "gt,aptc->apgc", sin_inner, paired_imag, precision=HIGH
    )
    freq_imag = jnp.einsum("gt,aptc->apgc", cos_inner, paired_imag, precision=HIGH) - jnp.einsum(
        "gt,aptc->apgc", sin_inner, paired_real, precision=HIGH
    )
    prod_real = freq_real[0] * freq_real[1] - freq_imag[0] * freq_imag[1]
    prod_imag = freq_real[0] * freq_imag[1] + freq_imag[0] * freq_real[1]
    final_factor = 1.0 / fft_length
    back_real = jnp.einsum("tg,pgc->ptc", cos_inner, prod_real, precision=HIGH) - jnp.einsum(
        "tg,pgc->ptc", sin_inner, prod_imag, precision=HIGH
    )
    back_imag = jnp.einsum("tg,pgc->ptc", cos_inner, prod_imag, precision=HIGH) + jnp.einsum(
        "tg,pgc->ptc", sin_inner, prod_real, precision=HIGH
    )
    returned = spread_out(jnp.stack([back_real, back_imag]))
    back_cos = cos_twist[:, :, None]
    back_sin = sin_twist[:, :, None]
    untwist_real = returned[0] * back_cos - returned[1] * back_sin
    untwist_imag = returned[0] * back_sin + returned[1] * back_cos
    time_values = jnp.einsum("ft,fjc->tjc", cos_outer, untwist_real, precision=HIGH) - jnp.einsum(
        "ft,fjc->tjc", sin_outer, untwist_imag, precision=HIGH
    )
    time_values = time_values * final_factor
    gathered = collect_in(time_values[None])
    return gathered[0, 0]


def transform_tables(blocks, rows):
    index = np.arange(rows)
    angle = 2.0 * np.pi * (index[:, None] * index[None, :] % rows) / rows
    cos, sin = np.cos(angle), np.sin(angle)
    there = np.block([[cos, sin], [-sin, cos]])
    back = np.block([[cos, -sin], [sin, cos]])
    twist = 2.0 * np.pi * np.arange(blocks + 1)[:, None] * index[None, :] / (2 * blocks * rows)
    twist = np.stack([np.cos(twist), np.sin(twist)], 1)[..., None]
    twist = np.broadcast_to(twist, twist.shape[:3] + (LANES,))
    return (
        jnp.asarray(there, jnp.bfloat16),
        jnp.asarray(back, jnp.bfloat16),
        jnp.asarray(twist, jnp.float32),
    )


def weighted(terms):
    total = None
    for factor, array in terms:
        if abs(factor) < 1e-12:
            continue
        if abs(factor - 1.0) < 1e-12:
            total = array if total is None else total + array
        elif abs(factor + 1.0) < 1e-12:
            total = -array if total is None else total - array
        else:
            total = factor * array if total is None else total + factor * array
    return total


def fold(load, blocks):
    half = blocks // 2
    first, middle = load(0), load(half)
    sums, gaps = [], []
    for j in range(1, half):
        low, high = load(j), load(blocks - j)
        sums.append(low + high)
        gaps.append(low - high)
    return first, middle, sums, gaps


def outer_stage(folded, freq, blocks):
    first, middle, sums, gaps = folded
    half = blocks // 2
    even = freq % 2 == 0
    cos_of = lambda j: math.cos(math.pi * freq * j / blocks)
    sin_of = lambda j: math.sin(math.pi * freq * j / blocks)
    with_cos, with_sin = (sums, gaps) if even else (gaps, sums)
    real = weighted(
        [(1.0, first), (cos_of(half), middle)] + [(cos_of(j), with_cos[j - 1]) for j in range(1, half)]
    )
    imag = weighted([(-sin_of(half), middle)] + [(-sin_of(j), with_sin[j - 1]) for j in range(1, half)])
    return real, imag


def twisted_stage(folded, freq, blocks, cos, sin):
    real, imag = outer_stage(folded, freq, blocks)
    if imag is None:
        return jnp.concatenate([real * cos, -(real * sin)], 0).astype(jnp.bfloat16)
    return jnp.concatenate([real * cos + imag * sin, imag * cos - real * sin], 0).astype(jnp.bfloat16)


def local_convolution(blocks, rows, load_signal, fil_real, fil_imag, there, back, twist):
    half = blocks // 2
    signal = fold(load_signal, blocks)
    cos_even, sin_even = [None] * (half + 1), [None] * (half + 1)
    cos_odd, sin_odd = [None] * (half + 1), [None] * (half + 1)
    plus = lambda old, new: new if old is None else (old if new is None else old + new)
    for freq in range(blocks + 1):
        cos, sin = twist[freq, 0], twist[freq, 1]
        stacked = twisted_stage(signal, freq, blocks, cos, sin)
        spectrum = jnp.dot(there[...], stacked, preferred_element_type=jnp.float32)
        sig_real, sig_imag = spectrum[:rows], spectrum[rows:]
        by_real, by_imag = fil_real[freq], fil_imag[freq]
        product = jnp.concatenate(
            [sig_real * by_real - sig_imag * by_imag, sig_real * by_imag + sig_imag * by_real], 0
        ).astype(jnp.bfloat16)
        values = jnp.dot(back[...], product, preferred_element_type=jnp.float32)
        real, imag = values[:rows], values[rows:]
        out_real, out_imag = real * cos - imag * sin, real * sin + imag * cos
        cos_sum, sin_sum = (cos_even, sin_even) if freq % 2 == 0 else (cos_odd, sin_odd)
        for j in range(half + 1):
            angle = math.pi * freq * j / blocks
            cos_sum[j] = plus(cos_sum[j], weighted([(math.cos(angle), out_real)]))
            sin_sum[j] = plus(sin_sum[j], weighted([(math.sin(angle), out_imag)]))
    minus = lambda left, right: left if right is None else (-right if left is None else left - right)
    result = [None] * blocks
    for j in range(half + 1):
        result[j] = minus(plus(cos_even[j], cos_odd[j]), plus(sin_even[j], sin_odd[j]))
        if 0 < j < half:
            result[blocks - j] = plus(minus(cos_even[j], cos_odd[j]), minus(sin_even[j], sin_odd[j]))
    return result


def whole_kernel(
    blocks, tokens, weight, taps, long_filter, skip, there, back, twist, out,
    held, slots, acc, rim_out, rim_in, query, gated,
    fil_out, fil_in, sig_out, sig_in, res_out, res_in, fil_real, fil_imag,
    weight_sem, token_send, token_recv, rim_send, rim_recv,
    fil_send, fil_recv, sig_send, sig_recv, res_send, res_recv,
):
    me, ch = lax.axis_index("seq"), lax.axis_index("ch")
    rows, width = tokens.shape
    pieces = held.shape[1]
    part = width // pieces
    wide = 2 * LANES
    chunks = blocks // 2
    level, side = me // 2, me % 2
    mate = ch + 1 - 2 * (ch % 2)
    across = (ch + 2) % 4
    across_mate = (mate + 2) % 4
    mesh_id = pl.DeviceIdType.MESH

    order = [(ch, None, q) for q in range(pieces)] + [(mate, 0, q) for q in range(pieces)]
    for q in range(pieces):
        order += [(across, 1, q), (across_mate, 2, q)]
    slot_count = slots.shape[0]

    def weight_copy(k):
        shard, _, q = order[k]
        first = pl.multiple_of(shard * width + q * part, part)
        return pltpu.make_async_copy(
            weight.at[:, pl.ds(first, part), :], slots.at[k % slot_count], weight_sem.at[k % slot_count]
        )

    def remote(src, dst, send, recv, **where):
        return pltpu.make_async_remote_copy(
            src_ref=src, dst_ref=dst, send_sem=send, recv_sem=recv, device_id=where, device_id_type=mesh_id
        )

    for k in range(slot_count):
        weight_copy(k).start()

    barrier = pltpu.get_barrier_semaphore()
    for far in range(1, blocks):
        pl.semaphore_signal(barrier, inc=1, device_id={"seq": (me + far) % blocks}, device_id_type=mesh_id)
    pl.semaphore_signal(barrier, inc=1, device_id={"ch": mate}, device_id_type=mesh_id)
    pl.semaphore_signal(barrier, inc=1, device_id={"ch": across}, device_id_type=mesh_id)
    for d in range(blocks):
        fil_out[d] = long_filter[:, d * LANES : (d + 1) * LANES].astype(jnp.bfloat16)
    pl.semaphore_wait(barrier, blocks + 1)

    own_piece = lambda q: tokens.at[:, q * part : (q + 1) * part]
    to_across = [
        remote(own_piece(q), held.at[1, q], token_send.at[1, q], token_recv.at[1, q], ch=across)
        for q in range(pieces)
    ]
    to_mate = [
        remote(own_piece(q), held.at[0, q], token_send.at[0, q], token_recv.at[0, q], ch=mate)
        for q in range(pieces)
    ]
    hand_on = [
        remote(held.at[1, q], held.at[2, q], token_send.at[2, q], token_recv.at[2, q], ch=mate)
        for q in range(pieces)
    ]

    def to_block(out_buf, in_buf, send, recv, d):
        return remote(out_buf.at[d], in_buf.at[me], send.at[d], recv.at[me], seq=d)

    def from_block(out_buf, in_buf, send, recv, d):
        return remote(out_buf.at[d], in_buf.at[d], send.at[d], recv.at[d], seq=d)

    fil = (fil_out, fil_in, fil_send, fil_recv)
    sig = (sig_out, sig_in, sig_send, sig_recv)
    res = (res_out, res_in, res_send, res_recv)
    for q in range(pieces):
        to_across[q].start()
        to_mate[q].start()
    for far in range(1, blocks):
        to_block(*fil, (me + far) % blocks).start()
    fil_in[me] = fil_out[me]

    def piece(k):
        _, place, q = order[k]
        return tokens[:, q * part : (q + 1) * part] if place is None else held[place, q]

    def product(k, chunk, j):
        columns = pl.ds(pl.multiple_of(chunk * wide, wide), wide)
        total = None
        for kk in (k, k + 1):
            term = jnp.dot(piece(kk), slots[kk % slot_count, j, :, columns], preferred_element_type=jnp.float32)
            total = term if total is None else total + term
        return total

    def arrive(k):
        for kk in (k, k + 1):
            _, place, q = order[kk]
            if place is not None:
                (to_mate, to_across, hand_on)[place][q].wait_recv()
            if place == 1:
                hand_on[q].start()
        for kk in (k, k + 1):
            weight_copy(kk).wait()

    def filter_spectrum():
        for far in range(1, blocks):
            from_block(*fil, (me + far) % blocks).wait_recv()
        folded = fold(lambda j: fil_in[j].astype(jnp.float32), blocks)
        for freq in range(blocks + 1):
            stacked = twisted_stage(folded, freq, blocks, twist[freq, 0], twist[freq, 1])
            spectrum = jnp.dot(there[...], stacked, preferred_element_type=jnp.float32)
            scale = (1.0 if freq in (0, blocks) else 2.0) / (2 * blocks * rows)
            fil_real[freq] = spectrum[:rows] * scale
            fil_imag[freq] = spectrum[rows:] * scale

    total_tiles = len(order)
    for k in range(0, total_tiles - 2, 2):
        arrive(k)

        def accumulate(n, carry, k=k):
            chunk, j = n // 3, n % 3
            value = product(k, chunk, j)
            if k == 0:
                acc[chunk, j, 8:, :] = value
            else:
                acc[chunk, j, 8:, :] += value
            return carry

        lax.fori_loop(0, 3 * chunks, accumulate, 0)
        for kk in (k, k + 1):
            if kk + slot_count < total_tiles:
                weight_copy(kk + slot_count).start()
        if k + 2 == 2 * pieces:
            filter_spectrum()
    last = total_tiles - 2
    arrive(last)

    chunk_of = lambda s: (level - s + chunks) % chunks
    following = (me + 1) % blocks

    def rim_copy(chunk):
        return remote(rim_out.at[chunk], rim_in.at[chunk], rim_send.at[chunk], rim_recv.at[chunk], seq=following)

    def project(s):
        chunk = chunk_of(s)

        def one(j, carry):
            value = (acc[chunk, j, 8:, :] + product(last, chunk, j)).astype(jnp.bfloat16)
            acc[chunk, j, 8:, :] = value.astype(jnp.float32)
            rim_out[chunk, j] = value[rows - 16 :]
            return carry

        lax.fori_loop(0, 3, one, 0)
        rim_copy(chunk).start()

    def short_filter(s):
        chunk = chunk_of(s)
        rim_copy(chunk).wait_recv()
        columns = pl.ds(pl.multiple_of(chunk * wide, wide), wide)
        results = []
        for j in range(3):
            rim = rim_in[chunk, j][8:].astype(jnp.float32)
            acc[chunk, j, :8, :] = jnp.where(me > 0, rim, 0.0)
            total = None
            for i in range(TAPS):
                term = taps[j, i : i + 1, columns] * acc[chunk, j, 8 - i : 8 - i + rows, :]
                total = term if total is None else total + term
            results.append(total)
        inputs = results[1] * results[2]
        for half in range(2):
            d = 2 * chunk + half
            lanes = slice(half * LANES, (half + 1) * LANES)
            query[d] = results[0][:, lanes]
            gated[d] = inputs[:, lanes]
            sig_out[d] = inputs[:, lanes].astype(jnp.bfloat16)
        if s == 0:
            to_block(*sig, 2 * level + 1 - side).start()
            sig_in[me] = sig_out[me]
        else:
            to_block(*sig, 2 * chunk).start()
            to_block(*sig, 2 * chunk + 1).start()

    for s in range(chunks):
        project(s)
        if s >= 2:
            short_filter(s - 1)
    short_filter(chunks - 1)
    short_filter(0)

    for far in range(1, blocks):
        from_block(*sig, (me + far) % blocks).wait_recv()
    result = local_convolution(
        blocks, rows, lambda j: sig_in[j].astype(jnp.float32), fil_real, fil_imag, there, back, twist
    )
    for j in range(blocks):
        res_out[j] = result[j].astype(jnp.bfloat16)
    for far in range(1, blocks):
        to_block(*res, (me + far) % blocks).start()
    res_in[me] = res_out[me]

    def finish(far, carry):
        d = (me + far) % blocks
        columns = pl.ds(pl.multiple_of(d * LANES, LANES), LANES)
        conv = res_in[d].astype(jnp.float32)
        out[:, columns] = (query[d] * (conv + skip[:, columns] * gated[d])).astype(jnp.bfloat16)
        return carry

    for far in range(blocks):
        if far:
            from_block(*res, (me + far) % blocks).wait_recv()
        finish(far, 0)

    for q in range(pieces):
        to_across[q].wait_send()
        to_mate[q].wait_send()
        hand_on[q].wait_send()
    for far in range(1, blocks):
        d = (me + far) % blocks
        to_block(*fil, d).wait_send()
        to_block(*sig, d).wait_send()
        to_block(*res, d).wait_send()
    for s in range(chunks):
        rim_copy(chunk_of(s)).wait_send()


def whole_operator(tokens, proj_weight, short_taps, long_filter, skip_gain):
    blocks = lax.axis_size("seq")
    rows, width = tokens.shape
    channels = proj_weight.shape[2]
    pieces = 4
    part = width // pieces
    chunks = blocks // 2
    lane_blocks = pltpu.VMEM((blocks, rows, LANES), jnp.bfloat16)
    lane_blocks_f32 = pltpu.VMEM((blocks, rows, LANES), jnp.float32)
    spectrum = pltpu.VMEM((blocks + 1, rows, LANES), jnp.float32)
    vmem = pl.BlockSpec(memory_space=pltpu.VMEM)
    slot_count = 8
    return pl.pallas_call(
        functools.partial(whole_kernel, blocks),
        out_shape=jax.ShapeDtypeStruct((rows, channels), jnp.bfloat16),
        in_specs=[vmem, pl.BlockSpec(memory_space=pl.ANY)] + [vmem] * 6,
        out_specs=vmem,
        scratch_shapes=[
            pltpu.VMEM((3, pieces, rows, part), jnp.bfloat16),
            pltpu.VMEM((slot_count, 3, part, channels), jnp.bfloat16),
            pltpu.VMEM((chunks, 3, rows + 8, 2 * LANES), jnp.float32),
            pltpu.VMEM((chunks, 3, 16, 2 * LANES), jnp.bfloat16),
            pltpu.VMEM((chunks, 3, 16, 2 * LANES), jnp.bfloat16),
            lane_blocks_f32,
            lane_blocks_f32,
        ]
        + [lane_blocks] * 6
        + [spectrum] * 2
        + [pltpu.SemaphoreType.DMA((slot_count,))]
        + [pltpu.SemaphoreType.DMA((3, pieces))] * 2
        + [pltpu.SemaphoreType.DMA((chunks,))] * 2
        + [pltpu.SemaphoreType.DMA((blocks,))] * 6,
        compiler_params=pltpu.CompilerParams(
            collective_id=0, has_side_effects=True, vmem_limit_bytes=58 * 1024 * 1024
        ),
        name="hyena_operator",
    )(
        tokens,
        proj_weight,
        short_taps,
        long_filter,
        skip_gain.reshape(1, channels),
        *transform_tables(blocks, rows),
    )


def per_device(tokens, proj_weight, short_taps, long_filter, skip_gain):
    row_count = tokens.shape[0]
    chan_count = proj_weight.shape[2]
    seq_count = lax.axis_size("seq")
    lane_tiles = chan_count == seq_count * LANES and seq_count % 4 == 0
    if lane_tiles and row_count % 16 == 0 and lax.axis_size("ch") == 4 and tokens.shape[1] % 512 == 0:
        return whole_operator(tokens, proj_weight, short_taps, long_filter, skip_gain)
    projected = jnp.einsum(
        "td,jdc->jtc",
        lax.all_gather(tokens, "ch", axis=1, tiled=True),
        proj_weight,
        preferred_element_type=jnp.float32,
    ).astype(jnp.bfloat16)
    rim_rows = shifted(projected[:, row_count - (TAPS - 1) :], "seq", 1)
    extended = jnp.concatenate([rim_rows, projected], 1)
    filtered = jnp.zeros((3, row_count, chan_count), jnp.float32)
    for tap_index in range(TAPS):
        begin = TAPS - 1 - tap_index
        filtered = filtered + short_taps[:, tap_index][:, None, :] * extended[
            :, begin : begin + row_count
        ].astype(jnp.float32)
    query_part = filtered[0]
    gated_input = filtered[1] * filtered[2]
    long_conv = spread_convolution(gated_input, long_filter)
    return (query_part * (long_conv + skip_gain * gated_input)).astype(jnp.bfloat16)


def solution(mesh):
    return jax.shard_map(
        per_device,
        mesh=mesh,
        in_specs=(
            P("seq", "ch"),
            P(None, None, "ch"),
            P(None, None, "ch"),
            P("seq", "ch"),
            P("ch"),
        ),
        out_specs=P("seq", "ch"),
        check_vma=False,
    )
```

```python
import functools
import math

import jax
import jax.numpy as jnp
import numpy as np
from jax import lax
from jax.experimental import pallas as pl
from jax.experimental.pallas import tpu as pltpu
from jax.sharding import PartitionSpec as P

TAPS = 7
LANES = 128


HIGH = lax.Precision.HIGHEST


def shifted(value, axis, by):
    size = lax.axis_size(axis)
    pairs = [(i, i + by) for i in range(size) if 0 <= i + by < size]
    return lax.ppermute(value, axis, pairs)


def spread_out(values):
    return lax.all_to_all(values, "seq", split_axis=2, concat_axis=1, tiled=True)


def collect_in(values):
    return lax.all_to_all(values, "seq", split_axis=1, concat_axis=2, tiled=True)


def angle_table(first, second, modulus):
    index_prod = first[:, None] * second[None, :] % modulus
    angles = index_prod.astype(jnp.float32) * (2.0 * math.pi / modulus)
    return (jnp.cos(angles), jnp.sin(angles))


def frequency_order(seq_count):
    places = jnp.arange(2 * seq_count, dtype=jnp.int32)
    owner = places // 2
    second = places % 2
    mirror = jnp.where(second == 0, owner, 2 * seq_count - owner)
    return jnp.where(owner == 0, second * seq_count, mirror)


def spread_convolution(signal, kernel):
    row_count = signal.shape[0]
    seq_count = lax.axis_size("seq")
    slice_rows = row_count // seq_count
    seq_total = seq_count * row_count
    fft_length = 2 * seq_total
    seq_index = lax.axis_index("seq")
    stacked = jnp.stack([signal, kernel])[:, None]
    spread = spread_out(stacked)
    freq_outer = frequency_order(seq_count)
    time_outer = jnp.arange(seq_count, dtype=jnp.int32)
    cos_outer, sin_outer = angle_table(freq_outer, time_outer, 2 * seq_count)
    inner_pos = seq_index * slice_rows + jnp.arange(slice_rows, dtype=jnp.int32)
    cos_twist, sin_twist = angle_table(freq_outer, inner_pos, fft_length)
    inner_index = jnp.arange(row_count, dtype=jnp.int32)
    cos_inner, sin_inner = angle_table(inner_index, inner_index, row_count)
    real_part = jnp.einsum("ft,atjc->afjc", cos_outer, spread, precision=HIGH)
    imag_part = -jnp.einsum("ft,atjc->afjc", sin_outer, spread, precision=HIGH)
    twist_cos = cos_twist[None, :, :, None]
    twist_sin = sin_twist[None, :, :, None]
    twisted_real = real_part * twist_cos + imag_part * twist_sin
    twisted_imag = imag_part * twist_cos - real_part * twist_sin
    paired = collect_in(jnp.concatenate([twisted_real, twisted_imag], 0))
    paired_real = paired[:2]
    paired_imag = paired[2:]
    freq_real = jnp.einsum("gt,aptc->apgc", cos_inner, paired_real, precision=HIGH) + jnp.einsum(
        "gt,aptc->apgc", sin_inner, paired_imag, precision=HIGH
    )
    freq_imag = jnp.einsum("gt,aptc->apgc", cos_inner, paired_imag, precision=HIGH) - jnp.einsum(
        "gt,aptc->apgc", sin_inner, paired_real, precision=HIGH
    )
    prod_real = freq_real[0] * freq_real[1] - freq_imag[0] * freq_imag[1]
    prod_imag = freq_real[0] * freq_imag[1] + freq_imag[0] * freq_real[1]
    final_factor = 1.0 / fft_length
    back_real = jnp.einsum("tg,pgc->ptc", cos_inner, prod_real, precision=HIGH) - jnp.einsum(
        "tg,pgc->ptc", sin_inner, prod_imag, precision=HIGH
    )
    back_imag = jnp.einsum("tg,pgc->ptc", cos_inner, prod_imag, precision=HIGH) + jnp.einsum(
        "tg,pgc->ptc", sin_inner, prod_real, precision=HIGH
    )
    returned = spread_out(jnp.stack([back_real, back_imag]))
    back_cos = cos_twist[:, :, None]
    back_sin = sin_twist[:, :, None]
    untwist_real = returned[0] * back_cos - returned[1] * back_sin
    untwist_imag = returned[0] * back_sin + returned[1] * back_cos
    time_values = jnp.einsum("ft,fjc->tjc", cos_outer, untwist_real, precision=HIGH) - jnp.einsum(
        "ft,fjc->tjc", sin_outer, untwist_imag, precision=HIGH
    )
    time_values = time_values * final_factor
    gathered = collect_in(time_values[None])
    return gathered[0, 0]


def transform_tables(blocks, rows):
    index = np.arange(rows)
    angle = 2.0 * np.pi * (index[:, None] * index[None, :] % rows) / rows
    cos, sin = np.cos(angle), np.sin(angle)
    there = np.block([[cos, sin], [-sin, cos]])
    back = np.block([[cos, -sin], [sin, cos]])
    twist = 2.0 * np.pi * np.arange(blocks + 1)[:, None] * index[None, :] / (2 * blocks * rows)
    twist = np.stack([np.cos(twist), np.sin(twist)], 1)[..., None]
    twist = np.broadcast_to(twist, twist.shape[:3] + (LANES,))
    return (
        jnp.asarray(there, jnp.bfloat16),
        jnp.asarray(back, jnp.bfloat16),
        jnp.asarray(twist, jnp.float32),
    )


def weighted(terms):
    total = None
    for factor, array in terms:
        if abs(factor) < 1e-12:
            continue
        if abs(factor - 1.0) < 1e-12:
            total = array if total is None else total + array
        elif abs(factor + 1.0) < 1e-12:
            total = -array if total is None else total - array
        else:
            total = factor * array if total is None else total + factor * array
    return total


def fold(load, blocks):
    half = blocks // 2
    first, middle = load(0), load(half)
    sums, gaps = [], []
    for j in range(1, half):
        low, high = load(j), load(blocks - j)
        sums.append(low + high)
        gaps.append(low - high)
    return first, middle, sums, gaps


def outer_stage(folded, freq, blocks):
    first, middle, sums, gaps = folded
    half = blocks // 2
    even = freq % 2 == 0
    cos_of = lambda j: math.cos(math.pi * freq * j / blocks)
    sin_of = lambda j: math.sin(math.pi * freq * j / blocks)
    with_cos, with_sin = (sums, gaps) if even else (gaps, sums)
    real = weighted(
        [(1.0, first), (cos_of(half), middle)] + [(cos_of(j), with_cos[j - 1]) for j in range(1, half)]
    )
    imag = weighted([(-sin_of(half), middle)] + [(-sin_of(j), with_sin[j - 1]) for j in range(1, half)])
    return real, imag


def twisted_stage(folded, freq, blocks, cos, sin):
    real, imag = outer_stage(folded, freq, blocks)
    if imag is None:
        return jnp.concatenate([real * cos, -(real * sin)], 0).astype(jnp.bfloat16)
    return jnp.concatenate([real * cos + imag * sin, imag * cos - real * sin], 0).astype(jnp.bfloat16)


def local_convolution(blocks, rows, load_signal, fil_real, fil_imag, there, back, twist):
    half = blocks // 2
    signal = fold(load_signal, blocks)
    cos_even, sin_even = [None] * (half + 1), [None] * (half + 1)
    cos_odd, sin_odd = [None] * (half + 1), [None] * (half + 1)
    plus = lambda old, new: new if old is None else (old if new is None else old + new)
    for freq in range(blocks + 1):
        cos, sin = twist[freq, 0], twist[freq, 1]
        stacked = twisted_stage(signal, freq, blocks, cos, sin)
        spectrum = jnp.dot(there[...], stacked, preferred_element_type=jnp.float32)
        sig_real, sig_imag = spectrum[:rows], spectrum[rows:]
        by_real, by_imag = fil_real[freq], fil_imag[freq]
        product = jnp.concatenate(
            [sig_real * by_real - sig_imag * by_imag, sig_real * by_imag + sig_imag * by_real], 0
        ).astype(jnp.bfloat16)
        values = jnp.dot(back[...], product, preferred_element_type=jnp.float32)
        real, imag = values[:rows], values[rows:]
        out_real, out_imag = real * cos - imag * sin, real * sin + imag * cos
        cos_sum, sin_sum = (cos_even, sin_even) if freq % 2 == 0 else (cos_odd, sin_odd)
        for j in range(half + 1):
            angle = math.pi * freq * j / blocks
            cos_sum[j] = plus(cos_sum[j], weighted([(math.cos(angle), out_real)]))
            sin_sum[j] = plus(sin_sum[j], weighted([(math.sin(angle), out_imag)]))
    minus = lambda left, right: left if right is None else (-right if left is None else left - right)
    result = [None] * blocks
    for j in range(half + 1):
        result[j] = minus(plus(cos_even[j], cos_odd[j]), plus(sin_even[j], sin_odd[j]))
        if 0 < j < half:
            result[blocks - j] = plus(minus(cos_even[j], cos_odd[j]), minus(sin_even[j], sin_odd[j]))
    return result


def whole_kernel(
    blocks, tokens, weight, taps, filter_hbm, skip, there_hbm, back_hbm, twist_hbm, out,
    long_filter, there, back, twist, own,
    held, slots, acc, rim_out, rim_in, query, gated,
    fil_out, fil_in, sig_out, sig_in, res_out, res_in, fil_real, fil_imag,
    input_sem, own_sem, weight_sem, token_send, token_recv, rim_send, rim_recv,
    fil_send, fil_recv, sig_send, sig_recv, res_send, res_recv,
):
    me, ch = lax.axis_index("seq"), lax.axis_index("ch")
    rows, width = tokens.shape
    pieces = held.shape[1]
    part = width // pieces
    wide = 2 * LANES
    chunks = blocks // 2
    level, side = me // 2, me % 2
    mate = ch + 1 - 2 * (ch % 2)
    across = (ch + 2) % 4
    across_mate = (mate + 2) % 4
    mesh_id = pl.DeviceIdType.MESH
    farthest_first = sorted(range(1, blocks), key=lambda far: abs(far - blocks // 2))

    order = [(ch, None, q) for q in range(pieces)] + [(mate, 0, q) for q in range(pieces)]
    for q in range(pieces):
        order += [(across, 1, q), (across_mate, 2, q)]
    slot_count = slots.shape[0]

    def weight_copy(k):
        shard, _, q = order[k]
        first = pl.multiple_of(shard * width + q * part, part)
        return pltpu.make_async_copy(
            weight.at[:, pl.ds(first, part), :], slots.at[k % slot_count], weight_sem.at[k % slot_count]
        )

    def remote(src, dst, send, recv, **where):
        return pltpu.make_async_remote_copy(
            src_ref=src, dst_ref=dst, send_sem=send, recv_sem=recv, device_id=where, device_id_type=mesh_id
        )

    filter_copy = pltpu.make_async_copy(filter_hbm, long_filter, input_sem.at[0])
    table_copies = [
        pltpu.make_async_copy(there_hbm, there, input_sem.at[1]),
        pltpu.make_async_copy(back_hbm, back, input_sem.at[2]),
        pltpu.make_async_copy(twist_hbm, twist, input_sem.at[3]),
    ]
    own_piece = lambda q: tokens.at[:, q * part : (q + 1) * part]
    own_copies = [pltpu.make_async_copy(own_piece(q), own.at[q], own_sem.at[q]) for q in range(pieces)]
    filter_copy.start()
    own_copies[0].start()
    own_copies[1].start()
    weight_copy(0).start()
    weight_copy(1).start()
    own_copies[2].start()
    own_copies[3].start()
    for k in range(2, slot_count):
        weight_copy(k).start()

    barrier = pltpu.get_barrier_semaphore()
    for far in range(1, blocks):
        pl.semaphore_signal(barrier, inc=1, device_id={"seq": (me + far) % blocks}, device_id_type=mesh_id)
    pl.semaphore_signal(barrier, inc=1, device_id={"ch": mate}, device_id_type=mesh_id)
    pl.semaphore_signal(barrier, inc=1, device_id={"ch": across}, device_id_type=mesh_id)
    filter_copy.wait()
    for d in range(blocks):
        fil_out[d] = long_filter[:, d * LANES : (d + 1) * LANES].astype(jnp.bfloat16)
    pl.semaphore_wait(barrier, blocks + 1)

    to_across = [
        remote(own_piece(q), held.at[1, q], token_send.at[1, q], token_recv.at[1, q], ch=across)
        for q in range(pieces)
    ]
    to_mate = [
        remote(own_piece(q), held.at[0, q], token_send.at[0, q], token_recv.at[0, q], ch=mate)
        for q in range(pieces)
    ]
    hand_on = [
        remote(held.at[1, q], held.at[2, q], token_send.at[2, q], token_recv.at[2, q], ch=mate)
        for q in range(pieces)
    ]

    def to_block(out_buf, in_buf, send, recv, d):
        return remote(out_buf.at[d], in_buf.at[me], send.at[d], recv.at[me], seq=d)

    def from_block(out_buf, in_buf, send, recv, d):
        return remote(out_buf.at[d], in_buf.at[d], send.at[d], recv.at[d], seq=d)

    fil = (fil_out, fil_in, fil_send, fil_recv)
    sig = (sig_out, sig_in, sig_send, sig_recv)
    res = (res_out, res_in, res_send, res_recv)
    to_across[0].start()
    for q in range(pieces):
        to_mate[q].start()
    to_across[1].start()
    for far in farthest_first:
        to_block(*fil, (me + far) % blocks).start()
    fil_in[me] = fil_out[me]

    def piece(k):
        _, place, q = order[k]
        return own[q] if place is None else held[place, q]

    def product(k, chunk, j):
        columns = pl.ds(pl.multiple_of(chunk * wide, wide), wide)
        total = None
        for kk in (k, k + 1):
            term = jnp.dot(piece(kk), slots[kk % slot_count, j, :, columns], preferred_element_type=jnp.float32)
            total = term if total is None else total + term
        return total

    def arrive(k):
        for kk in (k, k + 1):
            _, place, q = order[kk]
            if place is None:
                own_copies[q].wait()
            else:
                (to_mate, to_across, hand_on)[place][q].wait_recv()
            if place == 1:
                hand_on[q].start()
                if q + 2 < pieces:
                    to_across[q + 2].start()
        for kk in (k, k + 1):
            weight_copy(kk).wait()

    def filter_spectrum():
        for copy in table_copies:
            copy.wait()
        for far in range(1, blocks):
            from_block(*fil, (me + far) % blocks).wait_recv()
        folded = fold(lambda j: fil_in[j].astype(jnp.float32), blocks)
        for freq in range(blocks + 1):
            stacked = twisted_stage(folded, freq, blocks, twist[freq, 0], twist[freq, 1])
            spectrum = jnp.dot(there[...], stacked, preferred_element_type=jnp.float32)
            scale = (1.0 if freq in (0, blocks) else 2.0) / (2 * blocks * rows)
            fil_real[freq] = spectrum[:rows] * scale
            fil_imag[freq] = spectrum[rows:] * scale

    total_tiles = len(order)
    for k in range(0, total_tiles - 2, 2):
        arrive(k)

        def accumulate(n, carry, k=k):
            chunk, j = n // 3, n % 3
            value = product(k, chunk, j)
            if k == 0:
                acc[chunk, j, 8:, :] = value
            else:
                acc[chunk, j, 8:, :] += value
            return carry

        lax.fori_loop(0, 3 * chunks, accumulate, 0)
        for kk in (k, k + 1):
            if kk + slot_count < total_tiles:
                weight_copy(kk + slot_count).start()
        if k == slot_count:
            for copy in table_copies:
                copy.start()
    last = total_tiles - 2
    arrive(last)

    chunk_of = lambda s: (level - s + chunks) % chunks
    following = (me + 1) % blocks

    def rim_copy(chunk):
        return remote(rim_out.at[chunk], rim_in.at[chunk], rim_send.at[chunk], rim_recv.at[chunk], seq=following)

    def project(s):
        chunk = chunk_of(s)

        def one(j, carry):
            value = (acc[chunk, j, 8:, :] + product(last, chunk, j)).astype(jnp.bfloat16)
            acc[chunk, j, 8:, :] = value.astype(jnp.float32)
            rim_out[chunk, j] = value[rows - 16 :]
            return carry

        lax.fori_loop(0, 3, one, 0)
        rim_copy(chunk).start()

    def short_filter(s):
        chunk = chunk_of(s)
        rim_copy(chunk).wait_recv()
        columns = pl.ds(pl.multiple_of(chunk * wide, wide), wide)
        results = []
        for j in range(3):
            rim = rim_in[chunk, j][8:].astype(jnp.float32)
            acc[chunk, j, :8, :] = jnp.where(me > 0, rim, 0.0)
            total = None
            for i in range(TAPS):
                term = taps[j, i : i + 1, columns] * acc[chunk, j, 8 - i : 8 - i + rows, :]
                total = term if total is None else total + term
            results.append(total)
        inputs = results[1] * results[2]
        for half in range(2):
            d = 2 * chunk + half
            lanes = slice(half * LANES, (half + 1) * LANES)
            query[d] = results[0][:, lanes]
            gated[d] = inputs[:, lanes]
            sig_out[d] = inputs[:, lanes].astype(jnp.bfloat16)
        if s == 0:
            to_block(*sig, 2 * level + 1 - side).start()
            sig_in[me] = sig_out[me]
        else:
            to_block(*sig, 2 * chunk).start()
            to_block(*sig, 2 * chunk + 1).start()

    for s in range(chunks):
        project(s)
        if s >= 2:
            short_filter(s - 1)
    short_filter(chunks - 1)
    short_filter(0)
    filter_spectrum()

    for far in range(1, blocks):
        from_block(*sig, (me + far) % blocks).wait_recv()
    result = local_convolution(
        blocks, rows, lambda j: sig_in[j].astype(jnp.float32), fil_real, fil_imag, there, back, twist
    )
    for j in range(blocks):
        res_out[j] = result[j].astype(jnp.bfloat16)
    for far in farthest_first:
        to_block(*res, (me + far) % blocks).start()
    res_in[me] = res_out[me]

    def finish(far, carry):
        d = (me + far) % blocks
        columns = pl.ds(pl.multiple_of(d * LANES, LANES), LANES)
        conv = res_in[d].astype(jnp.float32)
        out[:, columns] = (query[d] * (conv + skip[:, columns] * gated[d])).astype(jnp.bfloat16)
        return carry

    for far in range(blocks):
        if far:
            from_block(*res, (me + far) % blocks).wait_recv()
        finish(far, 0)

    for q in range(pieces):
        to_across[q].wait_send()
        to_mate[q].wait_send()
        hand_on[q].wait_send()
    for far in range(1, blocks):
        d = (me + far) % blocks
        to_block(*fil, d).wait_send()
        to_block(*sig, d).wait_send()
        to_block(*res, d).wait_send()
    for s in range(chunks):
        rim_copy(chunk_of(s)).wait_send()


def whole_operator(tokens, proj_weight, short_taps, long_filter, skip_gain):
    blocks = lax.axis_size("seq")
    rows, width = tokens.shape
    channels = proj_weight.shape[2]
    pieces = 4
    part = width // pieces
    chunks = blocks // 2
    lane_blocks = pltpu.VMEM((blocks, rows, LANES), jnp.bfloat16)
    lane_blocks_f32 = pltpu.VMEM((blocks, rows, LANES), jnp.float32)
    spectrum = pltpu.VMEM((blocks + 1, rows, LANES), jnp.float32)
    vmem = pl.BlockSpec(memory_space=pltpu.VMEM)
    hbm = pl.BlockSpec(memory_space=pl.ANY)
    slot_count = 8
    tables = transform_tables(blocks, rows)
    return pl.pallas_call(
        functools.partial(whole_kernel, blocks),
        out_shape=jax.ShapeDtypeStruct((rows, channels), jnp.bfloat16),
        in_specs=[hbm, hbm, vmem, hbm, vmem, hbm, hbm, hbm],
        out_specs=vmem,
        scratch_shapes=[pltpu.VMEM(long_filter.shape, jnp.float32)]
        + [pltpu.VMEM(table.shape, table.dtype) for table in tables]
        + [
            pltpu.VMEM((pieces, rows, part), jnp.bfloat16),
            pltpu.VMEM((3, pieces, rows, part), jnp.bfloat16),
            pltpu.VMEM((slot_count, 3, part, channels), jnp.bfloat16),
            pltpu.VMEM((chunks, 3, rows + 8, 2 * LANES), jnp.float32),
            pltpu.VMEM((chunks, 3, 16, 2 * LANES), jnp.bfloat16),
            pltpu.VMEM((chunks, 3, 16, 2 * LANES), jnp.bfloat16),
            lane_blocks_f32,
            lane_blocks_f32,
        ]
        + [lane_blocks] * 6
        + [spectrum] * 2
        + [pltpu.SemaphoreType.DMA((4,)), pltpu.SemaphoreType.DMA((pieces,))]
        + [pltpu.SemaphoreType.DMA((slot_count,))]
        + [pltpu.SemaphoreType.DMA((3, pieces))] * 2
        + [pltpu.SemaphoreType.DMA((chunks,))] * 2
        + [pltpu.SemaphoreType.DMA((blocks,))] * 6,
        compiler_params=pltpu.CompilerParams(
            collective_id=0, has_side_effects=True, vmem_limit_bytes=58 * 1024 * 1024
        ),
        name="hyena_operator",
    )(
        tokens,
        proj_weight,
        short_taps,
        long_filter,
        skip_gain.reshape(1, channels),
        *tables,
    )


def per_device(tokens, proj_weight, short_taps, long_filter, skip_gain):
    row_count = tokens.shape[0]
    chan_count = proj_weight.shape[2]
    seq_count = lax.axis_size("seq")
    lane_tiles = chan_count == seq_count * LANES and seq_count % 4 == 0
    if lane_tiles and row_count % 16 == 0 and lax.axis_size("ch") == 4 and tokens.shape[1] % 512 == 0:
        return whole_operator(tokens, proj_weight, short_taps, long_filter, skip_gain)
    projected = jnp.einsum(
        "td,jdc->jtc",
        lax.all_gather(tokens, "ch", axis=1, tiled=True),
        proj_weight,
        preferred_element_type=jnp.float32,
    ).astype(jnp.bfloat16)
    rim_rows = shifted(projected[:, row_count - (TAPS - 1) :], "seq", 1)
    extended = jnp.concatenate([rim_rows, projected], 1)
    filtered = jnp.zeros((3, row_count, chan_count), jnp.float32)
    for tap_index in range(TAPS):
        begin = TAPS - 1 - tap_index
        filtered = filtered + short_taps[:, tap_index][:, None, :] * extended[
            :, begin : begin + row_count
        ].astype(jnp.float32)
    query_part = filtered[0]
    gated_input = filtered[1] * filtered[2]
    long_conv = spread_convolution(gated_input, long_filter)
    return (query_part * (long_conv + skip_gain * gated_input)).astype(jnp.bfloat16)


def solution(mesh):
    return jax.shard_map(
        per_device,
        mesh=mesh,
        in_specs=(
            P("seq", "ch"),
            P(None, None, "ch"),
            P(None, None, "ch"),
            P("seq", "ch"),
            P("ch"),
        ),
        out_specs=P("seq", "ch"),
        check_vma=False,
    )
```

```python
import functools
import math

import jax
import jax.numpy as jnp
import numpy as np
from jax import lax
from jax.experimental import pallas as pl
from jax.experimental.pallas import tpu as pltpu
from jax.sharding import PartitionSpec as P

TAPS = 7
LANES = 128


HIGH = lax.Precision.HIGHEST


def shifted(value, axis, by):
    size = lax.axis_size(axis)
    pairs = [(i, i + by) for i in range(size) if 0 <= i + by < size]
    return lax.ppermute(value, axis, pairs)


def spread_out(values):
    return lax.all_to_all(values, "seq", split_axis=2, concat_axis=1, tiled=True)


def collect_in(values):
    return lax.all_to_all(values, "seq", split_axis=1, concat_axis=2, tiled=True)


def angle_table(first, second, modulus):
    index_prod = first[:, None] * second[None, :] % modulus
    angles = index_prod.astype(jnp.float32) * (2.0 * math.pi / modulus)
    return (jnp.cos(angles), jnp.sin(angles))


def frequency_order(seq_count):
    places = jnp.arange(2 * seq_count, dtype=jnp.int32)
    owner = places // 2
    second = places % 2
    mirror = jnp.where(second == 0, owner, 2 * seq_count - owner)
    return jnp.where(owner == 0, second * seq_count, mirror)


def spread_convolution(signal, kernel):
    row_count = signal.shape[0]
    seq_count = lax.axis_size("seq")
    slice_rows = row_count // seq_count
    seq_total = seq_count * row_count
    fft_length = 2 * seq_total
    seq_index = lax.axis_index("seq")
    stacked = jnp.stack([signal, kernel])[:, None]
    spread = spread_out(stacked)
    freq_outer = frequency_order(seq_count)
    time_outer = jnp.arange(seq_count, dtype=jnp.int32)
    cos_outer, sin_outer = angle_table(freq_outer, time_outer, 2 * seq_count)
    inner_pos = seq_index * slice_rows + jnp.arange(slice_rows, dtype=jnp.int32)
    cos_twist, sin_twist = angle_table(freq_outer, inner_pos, fft_length)
    inner_index = jnp.arange(row_count, dtype=jnp.int32)
    cos_inner, sin_inner = angle_table(inner_index, inner_index, row_count)
    real_part = jnp.einsum("ft,atjc->afjc", cos_outer, spread, precision=HIGH)
    imag_part = -jnp.einsum("ft,atjc->afjc", sin_outer, spread, precision=HIGH)
    twist_cos = cos_twist[None, :, :, None]
    twist_sin = sin_twist[None, :, :, None]
    twisted_real = real_part * twist_cos + imag_part * twist_sin
    twisted_imag = imag_part * twist_cos - real_part * twist_sin
    paired = collect_in(jnp.concatenate([twisted_real, twisted_imag], 0))
    paired_real = paired[:2]
    paired_imag = paired[2:]
    freq_real = jnp.einsum("gt,aptc->apgc", cos_inner, paired_real, precision=HIGH) + jnp.einsum(
        "gt,aptc->apgc", sin_inner, paired_imag, precision=HIGH
    )
    freq_imag = jnp.einsum("gt,aptc->apgc", cos_inner, paired_imag, precision=HIGH) - jnp.einsum(
        "gt,aptc->apgc", sin_inner, paired_real, precision=HIGH
    )
    prod_real = freq_real[0] * freq_real[1] - freq_imag[0] * freq_imag[1]
    prod_imag = freq_real[0] * freq_imag[1] + freq_imag[0] * freq_real[1]
    final_factor = 1.0 / fft_length
    back_real = jnp.einsum("tg,pgc->ptc", cos_inner, prod_real, precision=HIGH) - jnp.einsum(
        "tg,pgc->ptc", sin_inner, prod_imag, precision=HIGH
    )
    back_imag = jnp.einsum("tg,pgc->ptc", cos_inner, prod_imag, precision=HIGH) + jnp.einsum(
        "tg,pgc->ptc", sin_inner, prod_real, precision=HIGH
    )
    returned = spread_out(jnp.stack([back_real, back_imag]))
    back_cos = cos_twist[:, :, None]
    back_sin = sin_twist[:, :, None]
    untwist_real = returned[0] * back_cos - returned[1] * back_sin
    untwist_imag = returned[0] * back_sin + returned[1] * back_cos
    time_values = jnp.einsum("ft,fjc->tjc", cos_outer, untwist_real, precision=HIGH) - jnp.einsum(
        "ft,fjc->tjc", sin_outer, untwist_imag, precision=HIGH
    )
    time_values = time_values * final_factor
    gathered = collect_in(time_values[None])
    return gathered[0, 0]


def transform_tables(blocks, rows):
    index = np.arange(rows)
    angle = 2.0 * np.pi * (index[:, None] * index[None, :] % rows) / rows
    cos, sin = np.cos(angle), np.sin(angle)
    there = np.block([[cos, sin], [-sin, cos]])
    back = np.block([[cos, -sin], [sin, cos]])
    twist = 2.0 * np.pi * np.arange(blocks + 1)[:, None] * index[None, :] / (2 * blocks * rows)
    twist = np.stack([np.cos(twist), np.sin(twist)], 1)[..., None]
    twist = np.broadcast_to(twist, twist.shape[:3] + (LANES,))
    return (
        jnp.asarray(there, jnp.bfloat16),
        jnp.asarray(back, jnp.bfloat16),
        jnp.asarray(twist, jnp.float32),
    )


def weighted(terms):
    total = None
    for factor, array in terms:
        if abs(factor) < 1e-12:
            continue
        if abs(factor - 1.0) < 1e-12:
            total = array if total is None else total + array
        elif abs(factor + 1.0) < 1e-12:
            total = -array if total is None else total - array
        else:
            total = factor * array if total is None else total + factor * array
    return total


def fold(load, blocks):
    half = blocks // 2
    first, middle = load(0), load(half)
    sums, gaps = [], []
    for j in range(1, half):
        low, high = load(j), load(blocks - j)
        sums.append(low + high)
        gaps.append(low - high)
    return first, middle, sums, gaps


def outer_stage(folded, freq, blocks):
    first, middle, sums, gaps = folded
    half = blocks // 2
    even = freq % 2 == 0
    cos_of = lambda j: math.cos(math.pi * freq * j / blocks)
    sin_of = lambda j: math.sin(math.pi * freq * j / blocks)
    with_cos, with_sin = (sums, gaps) if even else (gaps, sums)
    real = weighted(
        [(1.0, first), (cos_of(half), middle)] + [(cos_of(j), with_cos[j - 1]) for j in range(1, half)]
    )
    imag = weighted([(-sin_of(half), middle)] + [(-sin_of(j), with_sin[j - 1]) for j in range(1, half)])
    return real, imag


def twisted_stage(folded, freq, blocks, cos, sin):
    real, imag = outer_stage(folded, freq, blocks)
    if imag is None:
        return jnp.concatenate([real * cos, -(real * sin)], 0).astype(jnp.bfloat16)
    return jnp.concatenate([real * cos + imag * sin, imag * cos - real * sin], 0).astype(jnp.bfloat16)


def local_convolution(blocks, rows, load_signal, fil_real, fil_imag, there, back, twist):
    half = blocks // 2
    signal = fold(load_signal, blocks)
    cos_even, sin_even = [None] * (half + 1), [None] * (half + 1)
    cos_odd, sin_odd = [None] * (half + 1), [None] * (half + 1)
    plus = lambda old, new: new if old is None else (old if new is None else old + new)
    for freq in range(blocks + 1):
        cos, sin = twist[freq, 0], twist[freq, 1]
        stacked = twisted_stage(signal, freq, blocks, cos, sin)
        spectrum = jnp.dot(there[...], stacked, preferred_element_type=jnp.float32)
        sig_real, sig_imag = spectrum[:rows], spectrum[rows:]
        by_real, by_imag = fil_real[freq], fil_imag[freq]
        product = jnp.concatenate(
            [sig_real * by_real - sig_imag * by_imag, sig_real * by_imag + sig_imag * by_real], 0
        ).astype(jnp.bfloat16)
        values = jnp.dot(back[...], product, preferred_element_type=jnp.float32)
        real, imag = values[:rows], values[rows:]
        out_real, out_imag = real * cos - imag * sin, real * sin + imag * cos
        cos_sum, sin_sum = (cos_even, sin_even) if freq % 2 == 0 else (cos_odd, sin_odd)
        for j in range(half + 1):
            angle = math.pi * freq * j / blocks
            cos_sum[j] = plus(cos_sum[j], weighted([(math.cos(angle), out_real)]))
            sin_sum[j] = plus(sin_sum[j], weighted([(math.sin(angle), out_imag)]))
    minus = lambda left, right: left if right is None else (-right if left is None else left - right)
    result = [None] * blocks
    for j in range(half + 1):
        result[j] = minus(plus(cos_even[j], cos_odd[j]), plus(sin_even[j], sin_odd[j]))
        if 0 < j < half:
            result[blocks - j] = plus(minus(cos_even[j], cos_odd[j]), minus(sin_even[j], sin_odd[j]))
    return result


def whole_kernel(
    blocks, tokens, weight, taps, filter_hbm, skip, there_hbm, back_hbm, twist_hbm, out,
    long_filter, there, back, twist, own,
    held, slots, acc, rim_out, rim_in, query, gated,
    fil_out, fil_in, sig_out, sig_in, res_out, res_in, fil_real, fil_imag,
    input_sem, own_sem, weight_sem, token_send, token_recv, rim_send, rim_recv,
    fil_send, fil_recv, sig_send, sig_recv, res_send, res_recv,
):
    me, ch = lax.axis_index("seq"), lax.axis_index("ch")
    rows, width = tokens.shape
    pieces = held.shape[1]
    part = width // pieces
    wide = 2 * LANES
    chunks = blocks // 2
    level, side = me // 2, me % 2
    mate = ch + 1 - 2 * (ch % 2)
    across = (ch + 2) % 4
    across_mate = (mate + 2) % 4
    mesh_id = pl.DeviceIdType.MESH
    farthest_first = sorted(range(1, blocks), key=lambda far: abs(far - blocks // 2))

    order = [(ch, None, q) for q in range(pieces)] + [(mate, 0, q) for q in range(pieces)]
    for q in range(pieces):
        order += [(across, 1, q), (across_mate, 2, q)]
    slot_count = slots.shape[0]
    group = pieces
    strip_rows = 32

    def weight_copy(k):
        shard, _, q = order[k]
        first = pl.multiple_of(shard * width + q * part, part)
        return pltpu.make_async_copy(
            weight.at[:, pl.ds(first, part), :], slots.at[k % slot_count], weight_sem.at[k % slot_count]
        )

    def remote(src, dst, send, recv, **where):
        return pltpu.make_async_remote_copy(
            src_ref=src, dst_ref=dst, send_sem=send, recv_sem=recv, device_id=where, device_id_type=mesh_id
        )

    filter_copy = pltpu.make_async_copy(filter_hbm, long_filter, input_sem.at[0])
    table_copies = [
        pltpu.make_async_copy(there_hbm, there, input_sem.at[1]),
        pltpu.make_async_copy(back_hbm, back, input_sem.at[2]),
        pltpu.make_async_copy(twist_hbm, twist, input_sem.at[3]),
    ]
    own_piece = lambda q: tokens.at[:, q * part : (q + 1) * part]
    own_copies = [pltpu.make_async_copy(own_piece(q), own.at[q], own_sem.at[q]) for q in range(pieces)]
    filter_copy.start()
    own_copies[0].start()
    own_copies[1].start()
    weight_copy(0).start()
    weight_copy(1).start()
    own_copies[2].start()
    own_copies[3].start()
    for k in range(2, slot_count):
        weight_copy(k).start()

    barrier = pltpu.get_barrier_semaphore()
    for far in range(1, blocks):
        pl.semaphore_signal(barrier, inc=1, device_id={"seq": (me + far) % blocks}, device_id_type=mesh_id)
    pl.semaphore_signal(barrier, inc=1, device_id={"ch": mate}, device_id_type=mesh_id)
    pl.semaphore_signal(barrier, inc=1, device_id={"ch": across}, device_id_type=mesh_id)
    filter_copy.wait()
    for d in range(blocks):
        fil_out[d] = long_filter[:, d * LANES : (d + 1) * LANES].astype(jnp.bfloat16)
    pl.semaphore_wait(barrier, blocks + 1)

    to_across = [
        remote(own_piece(q), held.at[1, q], token_send.at[1, q], token_recv.at[1, q], ch=across)
        for q in range(pieces)
    ]
    to_mate = [
        remote(own_piece(q), held.at[0, q], token_send.at[0, q], token_recv.at[0, q], ch=mate)
        for q in range(pieces)
    ]
    hand_on = [
        remote(held.at[1, q], held.at[2, q], token_send.at[2, q], token_recv.at[2, q], ch=mate)
        for q in range(pieces)
    ]

    def to_block(out_buf, in_buf, send, recv, d):
        return remote(out_buf.at[d], in_buf.at[me], send.at[d], recv.at[me], seq=d)

    def from_block(out_buf, in_buf, send, recv, d):
        return remote(out_buf.at[d], in_buf.at[d], send.at[d], recv.at[d], seq=d)

    fil = (fil_out, fil_in, fil_send, fil_recv)
    sig = (sig_out, sig_in, sig_send, sig_recv)
    res = (res_out, res_in, res_send, res_recv)
    to_across[0].start()
    for q in range(pieces):
        to_mate[q].start()
    to_across[1].start()
    for far in farthest_first:
        to_block(*fil, (me + far) % blocks).start()
    fil_in[me] = fil_out[me]

    def piece(k):
        _, place, q = order[k]
        return own[q] if place is None else held[place, q]

    def product(k, chunk, j):
        columns = pl.ds(pl.multiple_of(chunk * wide, wide), wide)
        total = None
        for kk in range(k, k + group):
            term = jnp.dot(piece(kk), slots[kk % slot_count, j, :, columns], preferred_element_type=jnp.float32)
            total = term if total is None else total + term
        return total

    def arrive(k):
        for kk in range(k, k + group):
            _, place, q = order[kk]
            if place is None:
                own_copies[q].wait()
            else:
                (to_mate, to_across, hand_on)[place][q].wait_recv()
            if place == 1:
                hand_on[q].start()
                if q + 2 < pieces:
                    to_across[q + 2].start()
        for kk in range(k, k + group):
            weight_copy(kk).wait()

    def filter_spectrum():
        for copy in table_copies:
            copy.wait()
        for far in range(1, blocks):
            from_block(*fil, (me + far) % blocks).wait_recv()
        folded = fold(lambda j: fil_in[j].astype(jnp.float32), blocks)
        for freq in range(blocks + 1):
            stacked = twisted_stage(folded, freq, blocks, twist[freq, 0], twist[freq, 1])
            spectrum = jnp.dot(there[...], stacked, preferred_element_type=jnp.float32)
            scale = (1.0 if freq in (0, blocks) else 2.0) / (2 * blocks * rows)
            fil_real[freq] = spectrum[:rows] * scale
            fil_imag[freq] = spectrum[rows:] * scale

    total_tiles = len(order)
    for k in range(0, total_tiles - group, group):
        arrive(k)

        def accumulate(chunk, carry, k=k):
            for j in range(3):
                value = product(k, chunk, j)
                if k == 0:
                    acc[chunk, j, 8:, :] = value
                else:
                    acc[chunk, j, 8:, :] += value
            return carry

        lax.fori_loop(0, chunks, accumulate, 0)
        for kk in range(k, k + group):
            if kk + slot_count < total_tiles:
                weight_copy(kk + slot_count).start()
        if k == group:
            for copy in table_copies:
                copy.start()
    last = total_tiles - group
    arrive(last)

    chunk_of = lambda s: (level - s + chunks) % chunks
    following = (me + 1) % blocks

    def rim_copy(chunk):
        return remote(rim_out.at[chunk], rim_in.at[chunk], rim_send.at[chunk], rim_recv.at[chunk], seq=following)

    def project(s):
        chunk = chunk_of(s)

        for j in range(3):
            value = (acc[chunk, j, 8:, :] + product(last, chunk, j)).astype(jnp.bfloat16)
            acc[chunk, j, 8:, :] = value.astype(jnp.float32)
            rim_out[chunk, j] = value[rows - 16 :]
        rim_copy(chunk).start()

    def short_filter(s, first=False):
        chunk = chunk_of(s)
        rim_copy(chunk).wait_recv()
        columns = pl.ds(pl.multiple_of(chunk * wide, wide), wide)
        for j in range(3):
            rim = rim_in[chunk, j][8:].astype(jnp.float32)
            acc[chunk, j, :8, :] = jnp.where(me > 0, rim, 0.0)

        def strip(r, carry):
            begin = pl.multiple_of(r * strip_rows, strip_rows)
            results = []
            for j in range(3):
                window = acc[chunk, j, pl.ds(begin, strip_rows + 8), :]
                total = None
                for i in range(TAPS):
                    term = taps[j, i : i + 1, columns] * window[8 - i : 8 - i + strip_rows]
                    total = term if total is None else total + term
                results.append(total)
            inputs = results[1] * results[2]
            here = pl.ds(begin, strip_rows)
            for half in range(2):
                d = 2 * chunk + half
                lanes = slice(half * LANES, (half + 1) * LANES)
                query[d, here, :] = results[0][:, lanes]
                gated[d, here, :] = inputs[:, lanes]
                sig_out[d, here, :] = inputs[:, lanes].astype(jnp.bfloat16)
            return carry

        lax.fori_loop(0, rows // strip_rows, strip, 0)
        if first:
            to_block(*sig, 2 * level + 1 - side).start()
            sig_in[me] = sig_out[me]
        else:
            to_block(*sig, 2 * chunk).start()
            to_block(*sig, 2 * chunk + 1).start()

    def steps(begin, end, act):
        def body(s, carry):
            act(s)
            return carry

        lax.fori_loop(begin, end, body, 0)

    def both(s):
        project(s)
        short_filter(s - 1)

    steps(0, 2, project)
    steps(2, chunks, both)
    short_filter(chunks - 1)
    short_filter(0, first=True)
    filter_spectrum()

    for far in range(1, blocks):
        from_block(*sig, (me + far) % blocks).wait_recv()
    result = local_convolution(
        blocks, rows, lambda j: sig_in[j].astype(jnp.float32), fil_real, fil_imag, there, back, twist
    )
    for j in range(blocks):
        res_out[j] = result[j].astype(jnp.bfloat16)
    for far in farthest_first:
        to_block(*res, (me + far) % blocks).start()
    res_in[me] = res_out[me]

    def finish(far, carry):
        d = (me + far) % blocks
        columns = pl.ds(pl.multiple_of(d * LANES, LANES), LANES)
        conv = res_in[d].astype(jnp.float32)
        out[:, columns] = (query[d] * (conv + skip[:, columns] * gated[d])).astype(jnp.bfloat16)
        return carry

    for far in range(blocks):
        if far:
            from_block(*res, (me + far) % blocks).wait_recv()
        finish(far, 0)

    for q in range(pieces):
        to_across[q].wait_send()
        to_mate[q].wait_send()
        hand_on[q].wait_send()
    for far in range(1, blocks):
        d = (me + far) % blocks
        to_block(*fil, d).wait_send()
        to_block(*sig, d).wait_send()
        to_block(*res, d).wait_send()
    for s in range(chunks):
        rim_copy(chunk_of(s)).wait_send()


def whole_operator(tokens, proj_weight, short_taps, long_filter, skip_gain):
    blocks = lax.axis_size("seq")
    rows, width = tokens.shape
    channels = proj_weight.shape[2]
    pieces = 4
    part = width // pieces
    chunks = blocks // 2
    lane_blocks = pltpu.VMEM((blocks, rows, LANES), jnp.bfloat16)
    lane_blocks_f32 = pltpu.VMEM((blocks, rows, LANES), jnp.float32)
    spectrum = pltpu.VMEM((blocks + 1, rows, LANES), jnp.float32)
    vmem = pl.BlockSpec(memory_space=pltpu.VMEM)
    hbm = pl.BlockSpec(memory_space=pl.ANY)
    slot_count = 8
    tables = transform_tables(blocks, rows)
    return pl.pallas_call(
        functools.partial(whole_kernel, blocks),
        out_shape=jax.ShapeDtypeStruct((rows, channels), jnp.bfloat16),
        in_specs=[hbm, hbm, vmem, hbm, vmem, hbm, hbm, hbm],
        out_specs=vmem,
        scratch_shapes=[pltpu.VMEM(long_filter.shape, jnp.float32)]
        + [pltpu.VMEM(table.shape, table.dtype) for table in tables]
        + [
            pltpu.VMEM((pieces, rows, part), jnp.bfloat16),
            pltpu.VMEM((3, pieces, rows, part), jnp.bfloat16),
            pltpu.VMEM((slot_count, 3, part, channels), jnp.bfloat16),
            pltpu.VMEM((chunks, 3, rows + 8, 2 * LANES), jnp.float32),
            pltpu.VMEM((chunks, 3, 16, 2 * LANES), jnp.bfloat16),
            pltpu.VMEM((chunks, 3, 16, 2 * LANES), jnp.bfloat16),
            lane_blocks_f32,
            lane_blocks_f32,
        ]
        + [lane_blocks] * 6
        + [spectrum] * 2
        + [pltpu.SemaphoreType.DMA((4,)), pltpu.SemaphoreType.DMA((pieces,))]
        + [pltpu.SemaphoreType.DMA((slot_count,))]
        + [pltpu.SemaphoreType.DMA((3, pieces))] * 2
        + [pltpu.SemaphoreType.DMA((chunks,))] * 2
        + [pltpu.SemaphoreType.DMA((blocks,))] * 6,
        compiler_params=pltpu.CompilerParams(
            collective_id=0, has_side_effects=True, vmem_limit_bytes=58 * 1024 * 1024
        ),
        name="hyena_operator",
    )(
        tokens,
        proj_weight,
        short_taps,
        long_filter,
        skip_gain.reshape(1, channels),
        *tables,
    )


def per_device(tokens, proj_weight, short_taps, long_filter, skip_gain):
    row_count = tokens.shape[0]
    chan_count = proj_weight.shape[2]
    seq_count = lax.axis_size("seq")
    lane_tiles = chan_count == seq_count * LANES and seq_count % 4 == 0
    if lane_tiles and row_count % 32 == 0 and lax.axis_size("ch") == 4 and tokens.shape[1] % 512 == 0:
        return whole_operator(tokens, proj_weight, short_taps, long_filter, skip_gain)
    projected = jnp.einsum(
        "td,jdc->jtc",
        lax.all_gather(tokens, "ch", axis=1, tiled=True),
        proj_weight,
        preferred_element_type=jnp.float32,
    ).astype(jnp.bfloat16)
    rim_rows = shifted(projected[:, row_count - (TAPS - 1) :], "seq", 1)
    extended = jnp.concatenate([rim_rows, projected], 1)
    filtered = jnp.zeros((3, row_count, chan_count), jnp.float32)
    for tap_index in range(TAPS):
        begin = TAPS - 1 - tap_index
        filtered = filtered + short_taps[:, tap_index][:, None, :] * extended[
            :, begin : begin + row_count
        ].astype(jnp.float32)
    query_part = filtered[0]
    gated_input = filtered[1] * filtered[2]
    long_conv = spread_convolution(gated_input, long_filter)
    return (query_part * (long_conv + skip_gain * gated_input)).astype(jnp.bfloat16)


def solution(mesh):
    return jax.shard_map(
        per_device,
        mesh=mesh,
        in_specs=(
            P("seq", "ch"),
            P(None, None, "ch"),
            P(None, None, "ch"),
            P("seq", "ch"),
            P("ch"),
        ),
        out_specs=P("seq", "ch"),
        check_vma=False,
    )
```
